32 devices in a mesh: space: 16 (over z, x, core), ky: 2 (over y).
Axes of the slice: x: 2, y: 2, z: 4, core: 2. Of those that a mesh axis runs over, the one named last changes fastest.
Arguments:
- distribution: float32 [16, 128, 256, 128], P('space', 'ky'), may hold values from 0 to 2
- region: int32 [16, 256], P('space'), may hold values from 0 to 5, as said below
- region_doping: float32 [6], replicated, may hold values from -1 to 2
- region_relax: float32 [6], replicated, may hold values from 0.2 to 1
- equilibrium: float32 [128, 128], P('ky'), may hold values from 0.3 to 3
- kx_speed: float32 [128], replicated, may hold values from 0.1 to 1
- upwind_sign: int32 [128], replicated, may hold values from -1 to 1, as said below
Outputs:
- advanced: float32 [16, 128, 256, 128], P('space', 'ky')
The draws below stay inside these ranges and needn't reach their ends.
Inputs may be any that keep to these rules, and one draw needn't show every extreme that they name: region[x, y] = 2 band(y) + m[x, y], with m[x, y] 0 or 1 and band(y) = 0, 1, 2 on three runs of columns, each run at least 32 columns long. `upwind_sign`: exactly 64 entries are 1 and the others -1.
All inputs are finite; a program needn't handle non-finite values.
Results may differ from the reference program's by a relative error of at most 0.0003.
Values sent between devices are 32-bit elements; how exact they have to be, the bound alone decides.
A program may use at most 128 MiB of HBM per device.

```python
import math
import jax
import jax.numpy as jnp
from jax import lax

NY = 256
KX = 128
KY = 128
REGIONS = 6
NX = 16


def draw_region(key, part):
    first_key, second_key, third_key = jax.random.split(key, 3)
    lower = jax.random.randint(first_key, (), NY // 8, 3 * NY // 8)
    upper = jax.random.randint(second_key, (), 5 * NY // 8, 7 * NY // 8)
    column = jnp.arange(NY, dtype=jnp.int32)
    band_index = (column >= lower).astype(jnp.int32) + (column >= upper).astype(jnp.int32)
    material = jax.random.randint(third_key, (NX, NY), 0, 2)
    return (2 * band_index[None, :] + material).astype(jnp.int32)


def draw_upwind_sign(key, part):
    ordering = jax.random.permutation(key, KX)
    return jnp.where(ordering < KX // 2, 1, -1).astype(jnp.int32)


def block_scale(own_key, extent, shards, least, largest):
    loudness = 1.0
    for dim, shards_of in shards:
        steps = jax.random.uniform(jax.random.fold_in(jax.random.fold_in(own_key, 6), dim), (shards_of,), jnp.float32, least / len(shards), largest / len(shards))
        loudness = loudness * jnp.repeat(jnp.exp(steps), extent[dim] // shards_of).reshape((-1,) + (1,) * (len(extent) - 1 - dim))
    return loudness


def setup_inputs(seed: int = 0) -> dict:
    key_of = jax.random.split(jax.random.key(seed), 8)
    return {
        "distribution": jnp.clip(2.0 * jax.random.uniform(key_of[0], (NX, KY, NY, KX), jnp.float32) ** block_scale(key_of[0], (NX, KY, NY, KX), ((0, 16), (1, 2)), -0.2, 0.2), 0.0, 2.0),
        "region": draw_region(jax.random.fold_in(key_of[7], 71), 0),
        "region_doping": jnp.clip(jax.random.uniform(key_of[2], (REGIONS,), jnp.float32, -1.0, 2.0), -1.0, 2.0),
        "region_relax": jnp.clip(jnp.exp(jax.random.uniform(key_of[3], (REGIONS,), jnp.float32, math.log(0.2), math.log(1.0))), 0.2, 1.0),
        "equilibrium": jnp.clip(jnp.exp(math.log(3.0) - 2.3025851 * jax.random.uniform(key_of[4], (KY, KX), jnp.float32) ** block_scale(key_of[4], (KY, KX), ((0, 2),), -0.2, 0.2)), 0.3, 3.0),
        "kx_speed": jnp.clip(jnp.exp(jax.random.uniform(key_of[5], (KX,), jnp.float32, math.log(0.1), math.log(1.0))), 0.1, 1.0),
        "upwind_sign": draw_upwind_sign(jax.random.fold_in(key_of[7], 71), 0),
    }


COUPLING = 0.04
POISSON = 0.1
STEP = 0.4
DRIFT_Y = 0.8

def sine_table(length):
    positions = jnp.arange(1, length + 1, dtype=jnp.int32)
    phase_index = positions[:, None] * positions[None, :] % (2 * length + 2)
    return jnp.sqrt(2.0 / (length + 1.0)) * jnp.sin(math.pi * phase_index.astype(jnp.float32) / (length + 1.0))

def eigen_values(length):
    positions = jnp.arange(1, length + 1, dtype=jnp.int32).astype(jnp.float32)
    return 4.0 * jnp.sin(0.5 * math.pi * positions / (length + 1.0)) ** 2

def wigner_tables(modes):
    half_count = modes // 2
    shifts = jnp.arange(1, half_count + 1, dtype=jnp.int32)
    wave_index = jnp.arange(modes, dtype=jnp.int32)
    phase_index = shifts[:, None] * wave_index[None, :] % modes
    angles = 2.0 * math.pi / modes * phase_index.astype(jnp.float32)
    forward = jnp.concatenate([jnp.cos(angles), jnp.sin(angles)], axis=0)
    backward = jnp.concatenate([jnp.sin(angles).T, -jnp.cos(angles).T], axis=1)
    return (forward, backward)

def differences(potential, modes):
    half_count = modes // 2
    col_count = potential.shape[1]
    padded = jnp.pad(potential, ((0, 0), (half_count, half_count)))
    shifts = jnp.arange(1, half_count + 1, dtype=jnp.int32)
    column = jnp.arange(col_count, dtype=jnp.int32)
    ahead_vals = padded[:, half_count + column[None, :] + shifts[:, None]]
    behind = padded[:, half_count + column[None, :] - shifts[:, None]]
    return COUPLING * (ahead_vals - behind)

def lookup(region, values_table):
    classes = jnp.arange(values_table.shape[0], dtype=jnp.int32)
    return lax.optimization_barrier(jnp.sum(jnp.where(region[..., None] == classes, values_table, 0.0), axis=-1))

def reference(distribution, region, region_doping, region_relax, equilibrium, kx_speed, upwind_sign):
    precise = lax.Precision.HIGHEST
    row_count, ky_count, col_count, kx_count = distribution.shape
    density = lax.optimization_barrier(jnp.sum(distribution, axis=(1, 3))) / (ky_count * kx_count)
    doping = lookup(region, region_doping)
    relax_rate = lookup(region, region_relax)
    charge = density - doping
    sine_rows = sine_table(row_count)
    sine_cols = sine_table(col_count)
    spectral = jnp.dot(jnp.dot(sine_rows, charge, precision=precise), sine_cols, precision=precise)
    spectral = spectral / (eigen_values(row_count)[:, None] + eigen_values(col_count)[None, :])
    potential = POISSON * jnp.dot(jnp.dot(sine_rows, spectral, precision=precise), sine_cols, precision=precise)
    difference = differences(potential, ky_count)
    forward, backward = wigner_tables(ky_count)
    positive_kx = upwind_sign > 0
    ky_global = jnp.arange(ky_count, dtype=jnp.int32)
    upward = ky_global >= ky_count // 2
    vertical = DRIFT_Y * (ky_global.astype(jnp.float32) + 0.5 - 0.5 * ky_count) / (0.5 * ky_count)

    def one_row(inputs):
        position, weights, density_row, relax_row = inputs
        current = lax.dynamic_index_in_dim(distribution, position, 0, keepdims=False)
        before = lax.dynamic_index_in_dim(distribution, jnp.maximum(position - 1, 0), 0, keepdims=False)
        after = lax.dynamic_index_in_dim(distribution, jnp.minimum(position + 1, row_count - 1), 0, keepdims=False)
        before = jnp.where(position > 0, before, 0.0)
        after = jnp.where(position < row_count - 1, after, 0.0)
        upstream_x = jnp.where(positive_kx[None, None, :], before, after)
        drift_x = -kx_speed[None, None, :] * (current - upstream_x)
        zero_col = jnp.zeros_like(current[:, :1])
        from_low = jnp.concatenate([zero_col, current[:, :-1]], axis=1)
        from_high = jnp.concatenate([current[:, 1:], zero_col], axis=1)
        upstream_y = jnp.where(upward[:, None, None], from_low, from_high)
        drift_y = -jnp.abs(vertical)[:, None, None] * (current - upstream_y)
        flattened = current.reshape(ky_count, col_count * kx_count)
        coeffs = jnp.dot(forward, flattened, precision=precise).reshape(ky_count, col_count, kx_count)
        scaled = coeffs * jnp.concatenate([weights, weights], axis=0)[:, :, None]
        wigner = jnp.dot(backward, scaled.reshape(ky_count, col_count * kx_count), precision=precise)
        wigner = wigner.reshape(ky_count, col_count, kx_count)
        relaxation = relax_row[None, :, None] * (density_row[None, :, None] * equilibrium[:, None, :] - current)
        return current + STEP * (drift_x + drift_y + wigner + relaxation)
    positions = jnp.arange(row_count, dtype=jnp.int32)
    return lax.map(one_row, (positions, difference, density, relax_rate))
```

```python
import functools

import jax
import jax.numpy as jnp
import numpy as np
from jax import lax
from jax.experimental import pallas as pl
from jax.experimental.pallas import tpu as pltpu
from jax.sharding import PartitionSpec as P

COUPLING = 0.04
POISSON = 0.1
STEP = 0.4
DRIFT_Y = 0.8
WIDTH = 16
HALF = WIDTH // 2
EARLY = 2
MESH = pl.DeviceIdType.MESH
BF16 = jnp.bfloat16
F32 = jnp.float32


def sine_table(length):
    positions = np.arange(1, length + 1)
    phase = positions[:, None] * positions[None, :] % (2 * length + 2)
    return np.sqrt(2.0 / (length + 1.0)) * np.sin(np.pi * phase / (length + 1.0))


def eigen_values(length):
    positions = np.arange(1, length + 1)
    return 4.0 * np.sin(0.5 * np.pi * positions / (length + 1.0)) ** 2


def tables(rows, groups, modes, cols):
    half = modes // 2
    local = modes // groups
    phase = np.arange(1, half + 1)[:, None] * np.arange(modes)[None, :] % modes
    angles = 2.0 * np.pi / modes * phase
    forward = np.concatenate([np.cos(angles), np.sin(angles)], axis=0)
    backward = np.concatenate([np.sin(angles).T, -np.cos(angles).T], axis=1)
    by_owner = forward.reshape(modes, groups, local)
    forward_of = np.stack(
        [
            np.concatenate([by_owner[:, (g - p) % groups] for p in range(groups)], axis=1)
            for g in range(groups)
        ]
    )
    backward_of = backward.reshape(groups, local, modes)
    speed = DRIFT_Y * (np.arange(modes) + 0.5 - 0.5 * modes) / (0.5 * modes)
    speed_of = np.broadcast_to(speed.reshape(groups, local, 1), (groups, local, 128))
    sine_rows = sine_table(rows)
    expand = np.zeros((rows, rows, 8))
    expand[:, :, 0] = sine_rows
    own_row = np.broadcast_to(sine_rows[:, None, :], (rows, 8, rows))
    sine_cols = sine_table(cols)
    padded = np.pad(sine_cols, ((0, 0), (half, half)))
    pick = np.zeros((cols + 2 * half, 2 * half))
    centre = cols - 1 + half
    for s in range(1, half + 1):
        for column in (s - 1, half + s - 1):
            pick[centre + s, column] = 1.0
            pick[centre - s, column] = -1.0
    eigen = eigen_values(rows)[:, None] + eigen_values(cols)[None, :]
    every = (
        forward_of, backward_of, speed_of, expand.reshape(rows, rows * 8), own_row,
        sine_cols, padded, pick, eigen,
    )
    return [np.asarray(t, np.float32) for t in every]


def exact(a, b, contract=((1,), (0,))):
    return lax.dot_general(
        a, b, (contract, ((), ())), precision=lax.Precision.HIGHEST, preferred_element_type=F32
    )


def split(x):
    high = x.astype(BF16)
    return high, (x - high.astype(F32)).astype(BF16)


def triple(a, b):
    (a_high, a_low), (b_high, b_low) = a, b
    mul = functools.partial(jnp.dot, preferred_element_type=F32)
    return mul(a_high, b_high) + (mul(a_high, b_low) + mul(a_low, b_high))


def kernel(
    rows, groups,
    f_hbm, region_ref, doping_ref, relax_ref, eq_ref, speed_ref, sign_ref,
    forward_ref, backward_ref, vertical_ref, expand_ref, own_row_ref,
    sine_ref, padded_ref, pick_ref, eigen_ref,
    out_hbm,
    f_vm, spread, to_left, to_right, from_left, from_right, weight_high, weight_low,
    sums, parts, charges, diffs, dens, rate, up_x, result,
    load_sem, spread_send, spread_recv, part_send, part_recv, charge_send, charge_recv,
    left_send, left_recv, right_send, right_recv, out_sem,
):
    _, local, cols, kx = f_hbm.shape
    modes = local * groups
    chunks = cols // WIDTH
    row = lax.axis_index("space")
    group = lax.axis_index("ky")

    def other_group(p):
        return (row, lax.rem(group + p, groups))

    def other_row(i):
        return (lax.rem(row + i, rows), group)

    barrier = pltpu.get_barrier_semaphore()
    for p in range(1, groups):
        pl.semaphore_signal(barrier, inc=1, device_id=other_group(p), device_id_type=MESH)

    @pl.loop(1, rows)
    def _(i):
        pl.semaphore_signal(barrier, inc=1, device_id=other_row(i), device_id_type=MESH)

    def load(c):
        return pltpu.make_async_copy(
            f_hbm.at[0, :, pl.ds(pl.multiple_of(c * WIDTH, WIDTH), WIDTH), :],
            f_vm.at[c + 1], load_sem.at[c],
        )

    @pl.loop(0, chunks)
    def _(c):
        load(c).start()

    pl.semaphore_wait(barrier, rows + groups - 2)

    def spread_copy(p, c):
        return pltpu.make_async_remote_copy(
            src_ref=f_hbm.at[0, :, pl.ds(pl.multiple_of(c * WIDTH, WIDTH), WIDTH), :],
            dst_ref=spread.at[p - 1, c],
            send_sem=spread_send.at[p - 1, c], recv_sem=spread_recv.at[p - 1, c],
            device_id=other_group(p), device_id_type=MESH,
        )

    def part_copy(p):
        return pltpu.make_async_remote_copy(
            src_ref=parts.at[0], dst_ref=parts.at[p],
            send_sem=part_send.at[p - 1], recv_sem=part_recv.at[p - 1],
            device_id=other_group(p), device_id_type=MESH,
        )

    def charge_copy(i):
        return pltpu.make_async_remote_copy(
            src_ref=charges.at[0], dst_ref=charges.at[i],
            send_sem=charge_send.at[i - 1], recv_sem=charge_recv.at[i - 1],
            device_id=other_row(i), device_id_type=MESH,
        )

    def right_copy(c):
        return pltpu.make_async_remote_copy(
            src_ref=to_right.at[c], dst_ref=from_left.at[c],
            send_sem=right_send.at[c], recv_sem=right_recv.at[c],
            device_id=other_row(1), device_id_type=MESH,
        )

    def left_copy(c):
        return pltpu.make_async_remote_copy(
            src_ref=to_left.at[c], dst_ref=from_right.at[c],
            send_sem=left_send.at[c], recv_sem=left_recv.at[c],
            device_id=other_row(rows - 1), device_id_type=MESH,
        )

    for c in range(min(EARLY, chunks)):
        for p in range(1, groups):
            spread_copy(p, c).start()

    blank = jnp.zeros(f_vm.shape[1:], F32)
    f_vm[0] = blank
    f_vm[chunks + 1] = blank

    @pl.loop(0, chunks)
    def _(c):
        load(c).wait()
        sums[pl.ds(pl.multiple_of(c * WIDTH, WIDTH), WIDTH), :] = jnp.sum(f_vm[c + 1], axis=0)

    parts[0] = exact(jnp.ones((8, kx), F32), sums[...], ((1,), (1,))) / (modes * kx)
    for p in range(1, groups):
        part_copy(p).start()

    @pl.loop(min(EARLY, chunks), chunks)
    def _(c):
        for p in range(1, groups):
            spread_copy(p, c).start()

    lane = lax.broadcasted_iota(jnp.int32, (kx, kx), 1)
    place = lax.broadcasted_iota(jnp.int32, (kx, kx), 0)
    positive = jnp.broadcast_to(sign_ref[...] > 0, (kx, kx))
    ahead = exact(positive.astype(F32), (place < lane).astype(F32)).astype(jnp.int32)
    target = jnp.where(positive, ahead, kx // 2 + lane - ahead)
    first = (target == place).astype(F32)
    second = (lax.rem(target + kx // 2, kx) == place).astype(F32)
    low_lane = lax.broadcasted_iota(jnp.int32, (local * HALF, kx), 1) < kx // 2

    @pl.loop(0, chunks)
    def _(c):
        one = exact(f_vm[c + 1, :, :HALF, :].reshape(local * HALF, kx), first, ((1,), (1,)))
        two = exact(f_vm[c + 1, :, HALF:, :].reshape(local * HALF, kx), second, ((1,), (1,)))
        to_right[c] = jnp.where(low_lane, one, two).reshape(local, HALF, kx)
        to_left[c] = jnp.where(low_lane, two, one).reshape(local, HALF, kx)

    def lookup(table):
        region = jnp.broadcast_to(region_ref[...], (8, cols))
        value = jnp.zeros((8, cols), F32)
        for k in range(table.shape[0]):
            value = value + jnp.where(region == k, table[k], 0.0)
        return value

    def down(values):
        shape = (cols, cols)
        same = lax.broadcasted_iota(jnp.int32, shape, 0) == lax.broadcasted_iota(jnp.int32, shape, 1)
        spread_out = jnp.where(same, jnp.broadcast_to(values[:1], shape), 0.0)
        return exact(spread_out, jnp.ones((cols, kx), F32))

    rate[...] = down(lookup(relax_ref))
    for p in range(1, groups):
        part_copy(p).wait_recv()
    density = parts[0]
    for p in range(1, groups):
        density = density + parts[p]
    charges[0] = density - lookup(doping_ref)

    @pl.loop(1, rows)
    def _(i):
        charge_copy(i).start()

    @pl.loop(0, chunks)
    def _(c):
        @pl.when(row < rows - 1)
        def _():
            right_copy(c).start()

        @pl.when(row > 0)
        def _():
            left_copy(c).start()

    @pl.when(row == 0)
    def _():
        @pl.loop(0, chunks)
        def _(c):
            from_left[c] = jnp.zeros(from_left.shape[1:], F32)

    @pl.when(row == rows - 1)
    def _():
        @pl.loop(0, chunks)
        def _(c):
            from_right[c] = jnp.zeros(from_right.shape[1:], F32)

    dens[...] = down(density)

    @pl.loop(1, rows)
    def _(i):
        charge_copy(i).wait_recv()

    along_x = exact(expand_ref[row], charges[...].reshape(rows * 8, cols))
    spectral = exact(along_x, sine_ref[...]) / eigen_ref[...]
    own = exact(own_row_ref[row], spectral)
    potential = POISSON * exact(own, padded_ref[...])
    wide = jnp.broadcast_to(potential[:1], (cols, potential.shape[1]))
    shifted = pltpu.roll(wide, 0, 1, stride=1, stride_axis=0)
    diffs[...] = COUPLING * exact(shifted, pick_ref[...])

    forward = split(forward_ref[group])

    @pl.loop(0, chunks)
    def _(c):
        scaled = []
        for j in range(WIDTH):
            weights = diffs[pl.ds(cols - 1 - (c * WIDTH + j), 1), :]
            scaled.append(backward_ref[group] * weights)
        table = triple(split(jnp.concatenate(scaled, axis=0)), forward)
        high, low = split(table)
        weight_high[c] = high
        weight_low[c] = low

    f_rows = f_vm.reshape((chunks + 2) * local * WIDTH, kx)
    spread_rows = spread.reshape((groups - 1) * chunks * local * WIDTH, kx)
    up_rows = up_x.reshape(2 * local * HALF, kx)
    result_rows = result.reshape(2 * local * WIDTH, kx)

    def own_column(c, j):
        c, j = (c - 1, WIDTH - 1) if j < 0 else (c + 1, 0) if j == WIDTH else (c, j)
        return f_rows[pl.ds((c + 1) * (local * WIDTH) + j, local, stride=WIDTH), :]

    def out_copy(c):
        slot = lax.rem(c, 2)
        return pltpu.make_async_copy(
            result.at[slot],
            out_hbm.at[0, :, pl.ds(pl.multiple_of(c * WIDTH, WIDTH), WIDTH), :],
            out_sem.at[slot],
        )

    @pl.loop(0, chunks)
    def _(c):
        @pl.when(row > 0)
        def _():
            right_copy(c).wait_recv()

        @pl.when(row < rows - 1)
        def _():
            left_copy(c).wait_recv()

        left = from_left[c].reshape(local * HALF, kx)
        right = from_right[c].reshape(local * HALF, kx)
        up_x[0] = exact(jnp.where(low_lane, left, right), first).reshape(local, HALF, kx)
        up_x[1] = exact(jnp.where(low_lane, right, left), second).reshape(local, HALF, kx)

        @pl.when(c >= 2)
        def _():
            out_copy(c - 2).wait()

        for p in range(1, groups):
            spread_copy(p, c).wait_recv()

        vertical = vertical_ref[group]
        for j in range(WIDTH):
            current = own_column(c, j)
            every = [current]
            for p in range(groups - 1):
                start = (p * chunks + c) * (local * WIDTH) + j
                every.append(spread_rows[pl.ds(start, local, stride=WIDTH), :])
            picked = pl.ds(j * local, local)
            wigner = triple(
                (weight_high[c, picked, :], weight_low[c, picked, :]),
                split(jnp.concatenate(every, axis=0)),
            )
            half, inner = divmod(j, HALF)
            upstream_x = up_rows[pl.ds(half * local * HALF + inner, local, stride=HALF), :]
            upstream_y = jnp.where(vertical > 0, own_column(c, j - 1), own_column(c, j + 1))
            drift_x = -speed_ref[...] * (current - upstream_x)
            drift_y = -jnp.abs(vertical) * (current - upstream_y)
            column = pl.ds(c * WIDTH + j, 1)
            relaxation = rate[column, :] * (dens[column, :] * eq_ref[...] - current)
            total = current + STEP * (drift_x + drift_y + wigner + relaxation)
            slot = lax.rem(c, 2)
            result_rows[pl.ds(slot * (local * WIDTH) + j, local, stride=WIDTH), :] = total
        out_copy(c).start()

    for c in range(max(chunks - 2, 0), chunks):
        out_copy(c).wait()

    for p in range(1, groups):
        part_copy(p).wait_send()

        @pl.loop(0, chunks)
        def _(c):
            spread_copy(p, c).wait_send()

    @pl.loop(1, rows)
    def _(i):
        charge_copy(i).wait_send()

    @pl.loop(0, chunks)
    def _(c):
        @pl.when(row < rows - 1)
        def _():
            right_copy(c).wait_send()

        @pl.when(row > 0)
        def _():
            left_copy(c).wait_send()


def shards(rows, groups, distribution, region, doping, relax, equilibrium, speed, sign):
    _, local, cols, kx = distribution.shape
    modes = local * groups
    chunks = cols // WIDTH
    consts = tables(rows, groups, modes, cols)
    expand = consts[3].reshape(rows, rows, 8)
    order = (np.arange(rows)[:, None] - np.arange(rows)[None, :]) % rows
    consts[3] = np.stack([expand[:, order[r]].reshape(rows, rows * 8) for r in range(rows)])
    vmem = pl.BlockSpec(memory_space=pltpu.VMEM)
    smem = pl.BlockSpec(memory_space=pltpu.SMEM)
    hbm = pl.BlockSpec(memory_space=pl.ANY)
    piece = (local, WIDTH, kx)
    halo = (chunks, local, HALF, kx)
    dma = pltpu.SemaphoreType.DMA
    return pl.pallas_call(
        functools.partial(kernel, rows, groups),
        out_shape=jax.ShapeDtypeStruct(distribution.shape, F32),
        in_specs=[hbm, vmem, smem, smem] + [vmem] * (3 + len(consts)),
        out_specs=hbm,
        scratch_shapes=[
            pltpu.VMEM((chunks + 2,) + piece, F32),
            pltpu.VMEM((groups - 1, chunks) + piece, F32),
            pltpu.VMEM(halo, F32),
            pltpu.VMEM(halo, F32),
            pltpu.VMEM(halo, F32),
            pltpu.VMEM(halo, F32),
            pltpu.VMEM((chunks, local * WIDTH, modes), BF16),
            pltpu.VMEM((chunks, local * WIDTH, modes), BF16),
            pltpu.VMEM((cols, kx), F32),
            pltpu.VMEM((groups, 8, cols), F32),
            pltpu.VMEM((rows, 8, cols), F32),
            pltpu.VMEM((cols, modes), F32),
            pltpu.VMEM((cols, kx), F32),
            pltpu.VMEM((cols, kx), F32),
            pltpu.VMEM((2, local, HALF, kx), F32),
            pltpu.VMEM((2,) + piece, F32),
            dma((chunks,)),
            dma((groups - 1, chunks)),
            dma((groups - 1, chunks)),
            dma((groups - 1,)),
            dma((groups - 1,)),
            dma((rows - 1,)),
            dma((rows - 1,)),
            dma((chunks,)),
            dma((chunks,)),
            dma((chunks,)),
            dma((chunks,)),
            dma((2,)),
        ],
        compiler_params=pltpu.CompilerParams(
            collective_id=0, has_side_effects=True, vmem_limit_bytes=56 * 1024 * 1024
        ),
        cost_estimate=pl.CostEstimate(
            flops=2 * modes * local * cols * kx * 6,
            bytes_accessed=8 * local * cols * kx,
            transcendentals=0,
        ),
    )(
        distribution, region, doping, relax, equilibrium,
        speed.reshape(1, kx), sign.reshape(1, kx), *consts,
    )


def solution(mesh):
    return jax.shard_map(
        functools.partial(shards, mesh.shape["space"], mesh.shape["ky"]),
        mesh=mesh,
        in_specs=(
            P("space", "ky", None, None),
            P("space", None),
            P(),
            P(),
            P("ky", None),
            P(),
            P(),
        ),
        out_specs=P("space", "ky", None, None),
        check_vma=False,
    )
```

```python
import functools

import jax
import jax.numpy as jnp
import numpy as np
from jax import lax
from jax.experimental import pallas as pl
from jax.experimental.pallas import tpu as pltpu
from jax.sharding import PartitionSpec as P

COUPLING = 0.04
POISSON = 0.1
STEP = 0.4
DRIFT_Y = 0.8
WIDTH = 16
HALF = WIDTH // 2
EARLY = 2
TABLES = 9
MESH = pl.DeviceIdType.MESH
BF16 = jnp.bfloat16
F32 = jnp.float32


def sine_table(length):
    positions = np.arange(1, length + 1)
    phase = positions[:, None] * positions[None, :] % (2 * length + 2)
    return np.sqrt(2.0 / (length + 1.0)) * np.sin(np.pi * phase / (length + 1.0))


def eigen_values(length):
    positions = np.arange(1, length + 1)
    return 4.0 * np.sin(0.5 * np.pi * positions / (length + 1.0)) ** 2


def tables(rows, groups, modes, cols):
    half = modes // 2
    local = modes // groups
    phase = np.arange(1, half + 1)[:, None] * np.arange(modes)[None, :] % modes
    angles = 2.0 * np.pi / modes * phase
    forward = np.concatenate([np.cos(angles), np.sin(angles)], axis=0)
    backward = np.concatenate([np.sin(angles).T, -np.cos(angles).T], axis=1)
    by_owner = forward.reshape(modes, groups, local)
    forward_of = np.stack(
        [
            np.concatenate([by_owner[:, (g - p) % groups] for p in range(groups)], axis=1)
            for g in range(groups)
        ]
    )
    backward_of = backward.reshape(groups, local, modes)
    speed = DRIFT_Y * (np.arange(modes) + 0.5 - 0.5 * modes) / (0.5 * modes)
    speed_of = np.broadcast_to(speed.reshape(groups, local, 1), (groups, local, 128))
    sine_rows = sine_table(rows)
    expand = np.zeros((rows, rows, 8))
    expand[:, :, 0] = sine_rows
    own_row = np.broadcast_to(sine_rows[:, None, :], (rows, 8, rows))
    sine_cols = sine_table(cols)
    padded = np.pad(sine_cols, ((0, 0), (half, half)))
    pick = np.zeros((cols + 2 * half, 2 * half))
    centre = cols - 1 + half
    for s in range(1, half + 1):
        for column in (s - 1, half + s - 1):
            pick[centre + s, column] = 1.0
            pick[centre - s, column] = -1.0
    eigen = eigen_values(rows)[:, None] + eigen_values(cols)[None, :]
    every = (
        forward_of, backward_of, speed_of, expand.reshape(rows, rows * 8), own_row,
        sine_cols, padded, pick, eigen,
    )
    return [np.asarray(t, np.float32) for t in every]


def exact(a, b, contract=((1,), (0,))):
    return lax.dot_general(
        a, b, (contract, ((), ())), precision=lax.Precision.HIGHEST, preferred_element_type=F32
    )


def split(x):
    high = x.astype(BF16)
    return high, (x - high.astype(F32)).astype(BF16)


def triple(a, b):
    (a_high, a_low), (b_high, b_low) = a, b
    mul = functools.partial(jnp.dot, preferred_element_type=F32)
    return mul(a_high, b_high) + (mul(a_high, b_low) + mul(a_low, b_high))


def kernel(
    rows, groups,
    f_hbm, region_ref, doping_ref, relax_ref, eq_ref, speed_ref, sign_ref,
    *refs,
):
    table_sources, out_ref, table_refs = refs[:TABLES], refs[TABLES], refs[TABLES + 1:2 * TABLES + 1]
    (
        forward_ref, backward_ref, vertical_ref, expand_ref, own_row_ref,
        sine_ref, padded_ref, pick_ref, eigen_ref,
    ) = table_refs
    (
        f_vm, spread, to_left, to_right, from_left, from_right, weight_high, weight_low,
        sums, parts, charges, diffs, dens, rate, up_x,
        load_sem, spread_send, spread_recv, part_send, part_recv, charge_send, charge_recv,
        left_send, left_recv, right_send, right_recv, table_sem,
    ) = refs[2 * TABLES + 1:]
    _, local, cols, kx = f_hbm.shape
    modes = local * groups
    chunks = cols // WIDTH
    last = chunks - 1
    row = lax.axis_index("space")
    group = lax.axis_index("ky")

    def other_group(p):
        return (row, lax.rem(group + p, groups))

    def other_row(i):
        return (lax.rem(row + i, rows), group)

    barrier = pltpu.get_barrier_semaphore()
    for p in range(1, groups):
        pl.semaphore_signal(barrier, inc=1, device_id=other_group(p), device_id_type=MESH)

    @pl.loop(1, rows)
    def _(i):
        pl.semaphore_signal(barrier, inc=1, device_id=other_row(i), device_id_type=MESH)

    def load(c):
        return pltpu.make_async_copy(
            f_hbm.at[0, :, pl.ds(pl.multiple_of(c * WIDTH, WIDTH), WIDTH), :],
            f_vm.at[c + 1], load_sem.at[c],
        )

    @pl.loop(0, chunks)
    def _(c):
        load(c).start()

    pl.semaphore_wait(barrier, rows + groups - 2)

    def spread_copy(p, c, half=None):
        first_col = pl.multiple_of(c * WIDTH, WIDTH)
        place, target, sem = pl.ds(first_col, WIDTH), spread.at[p - 1, c], c
        if half is not None:
            place = pl.ds(last * WIDTH + half * HALF, HALF)
            target, sem = spread.at[p - 1, last, :, pl.ds(half * HALF, HALF), :], last + half
        return pltpu.make_async_remote_copy(
            src_ref=f_hbm.at[0, :, place, :],
            dst_ref=target,
            send_sem=spread_send.at[p - 1, sem], recv_sem=spread_recv.at[p - 1, sem],
            device_id=other_group(p), device_id_type=MESH,
        )

    def part_copy(p):
        return pltpu.make_async_remote_copy(
            src_ref=parts.at[0], dst_ref=parts.at[p],
            send_sem=part_send.at[p - 1], recv_sem=part_recv.at[p - 1],
            device_id=other_group(p), device_id_type=MESH,
        )

    def charge_copy(i):
        return pltpu.make_async_remote_copy(
            src_ref=charges.at[0], dst_ref=charges.at[i],
            send_sem=charge_send.at[i - 1], recv_sem=charge_recv.at[i - 1],
            device_id=other_row(i), device_id_type=MESH,
        )

    def right_copy(c):
        return pltpu.make_async_remote_copy(
            src_ref=to_right.at[c], dst_ref=from_left.at[c],
            send_sem=right_send.at[c], recv_sem=right_recv.at[c],
            device_id=other_row(1), device_id_type=MESH,
        )

    def left_copy(c):
        return pltpu.make_async_remote_copy(
            src_ref=to_left.at[c], dst_ref=from_right.at[c],
            send_sem=left_send.at[c], recv_sem=left_recv.at[c],
            device_id=other_row(rows - 1), device_id_type=MESH,
        )

    for c in range(min(EARLY, last)):
        for p in range(1, groups):
            spread_copy(p, c).start()

    table_copies = [
        pltpu.make_async_copy(source, table, table_sem.at[i])
        for i, (source, table) in enumerate(zip(table_sources, table_refs))
    ]
    for copy in table_copies:
        copy.start()

    blank = jnp.zeros(f_vm.shape[1:], F32)
    f_vm[0] = blank
    f_vm[chunks + 1] = blank

    @pl.loop(0, chunks)
    def _(c):
        load(c).wait()
        sums[pl.ds(pl.multiple_of(c * WIDTH, WIDTH), WIDTH), :] = jnp.sum(f_vm[c + 1], axis=0)

    parts[0] = exact(jnp.ones((8, kx), F32), sums[...], ((1,), (1,))) / (modes * kx)
    for p in range(1, groups):
        part_copy(p).start()

    @pl.loop(min(EARLY, last), last)
    def _(c):
        for p in range(1, groups):
            spread_copy(p, c).start()

    for half in range(2):
        for p in range(1, groups):
            spread_copy(p, last, half).start()

    lane = lax.broadcasted_iota(jnp.int32, (kx, kx), 1)
    place = lax.broadcasted_iota(jnp.int32, (kx, kx), 0)
    positive = jnp.broadcast_to(sign_ref[...] > 0, (kx, kx))
    ahead = exact(positive.astype(F32), (place < lane).astype(F32)).astype(jnp.int32)
    target = jnp.where(positive, ahead, kx // 2 + lane - ahead)
    first = (target == place).astype(F32)
    second = (lax.rem(target + kx // 2, kx) == place).astype(F32)
    low_lane = lax.broadcasted_iota(jnp.int32, (local * HALF, kx), 1) < kx // 2

    @pl.loop(0, chunks)
    def _(c):
        one = exact(f_vm[c + 1, :, :HALF, :].reshape(local * HALF, kx), first, ((1,), (1,)))
        two = exact(f_vm[c + 1, :, HALF:, :].reshape(local * HALF, kx), second, ((1,), (1,)))
        to_right[c] = jnp.where(low_lane, one, two).reshape(local, HALF, kx)
        to_left[c] = jnp.where(low_lane, two, one).reshape(local, HALF, kx)

    def lookup(table):
        region = jnp.broadcast_to(region_ref[...], (8, cols))
        value = jnp.zeros((8, cols), F32)
        for k in range(table.shape[0]):
            value = value + jnp.where(region == k, table[k], 0.0)
        return value

    def down(values):
        shape = (cols, cols)
        same = lax.broadcasted_iota(jnp.int32, shape, 0) == lax.broadcasted_iota(jnp.int32, shape, 1)
        spread_out = jnp.where(same, jnp.broadcast_to(values[:1], shape), 0.0)
        return exact(spread_out, jnp.ones((cols, kx), F32))

    rate[...] = down(lookup(relax_ref))
    for p in range(1, groups):
        part_copy(p).wait_recv()
    density = parts[0]
    for p in range(1, groups):
        density = density + parts[p]
    charges[0] = density - lookup(doping_ref)

    @pl.loop(1, rows)
    def _(i):
        charge_copy(i).start()

    @pl.loop(0, chunks)
    def _(c):
        @pl.when(row < rows - 1)
        def _():
            right_copy(c).start()

        @pl.when(row > 0)
        def _():
            left_copy(c).start()

    @pl.when(row == 0)
    def _():
        @pl.loop(0, chunks)
        def _(c):
            from_left[c] = jnp.zeros(from_left.shape[1:], F32)

    @pl.when(row == rows - 1)
    def _():
        @pl.loop(0, chunks)
        def _(c):
            from_right[c] = jnp.zeros(from_right.shape[1:], F32)

    dens[...] = down(density)
    for copy in table_copies:
        copy.wait()

    @pl.loop(1, rows)
    def _(i):
        charge_copy(i).wait_recv()

    along_x = exact(expand_ref[row], charges[...].reshape(rows * 8, cols))
    spectral = exact(along_x, sine_ref[...]) / eigen_ref[...]
    own = exact(own_row_ref[row], spectral)
    potential = POISSON * exact(own, padded_ref[...])
    wide = jnp.broadcast_to(potential[:1], (cols, potential.shape[1]))
    shifted = pltpu.roll(wide, 0, 1, stride=1, stride_axis=0)
    diffs[...] = COUPLING * exact(shifted, pick_ref[...])

    forward = split(forward_ref[group])

    @pl.loop(0, chunks)
    def _(c):
        scaled = []
        for j in range(WIDTH):
            weights = diffs[pl.ds(cols - 1 - (c * WIDTH + j), 1), :]
            scaled.append(backward_ref[group] * weights)
        table = triple(split(jnp.concatenate(scaled, axis=0)), forward)
        high, low = split(table)
        weight_high[c] = high
        weight_low[c] = low

    f_rows = f_vm.reshape((chunks + 2) * local * WIDTH, kx)
    spread_rows = spread.reshape((groups - 1) * chunks * local * WIDTH, kx)
    up_rows = up_x.reshape(2 * local * HALF, kx)
    out_rows = out_ref.reshape(local * cols, kx)

    def nonlocal_part(c, j, values, start):
        count = values[0].shape[0]
        blank_before = [jnp.zeros((start, kx), BF16)] if start else []
        rest = modes - start - count
        blank_after = [jnp.zeros((rest, kx), BF16)] if rest else []
        padded = [jnp.concatenate(blank_before + [v] + blank_after, axis=0) for v in values]
        picked = pl.ds(j * local, local)
        return triple((weight_high[c, picked, :], weight_low[c, picked, :]), padded)

    def own_column(c, j):
        c, j = (c - 1, WIDTH - 1) if j < 0 else (c + 1, 0) if j == WIDTH else (c, j)
        return f_rows[pl.ds((c + 1) * (local * WIDTH) + j, local, stride=WIDTH), :]

    def advance(c, halves):
        @pl.when(row > 0)
        def _():
            right_copy(c).wait_recv()

        @pl.when(row < rows - 1)
        def _():
            left_copy(c).wait_recv()

        left = from_left[c].reshape(local * HALF, kx)
        right = from_right[c].reshape(local * HALF, kx)
        up_x[0] = exact(jnp.where(low_lane, left, right), first).reshape(local, HALF, kx)
        up_x[1] = exact(jnp.where(low_lane, right, left), second).reshape(local, HALF, kx)

        vertical = vertical_ref[group]
        for j in range(WIDTH):
            current = own_column(c, j)
            wigner = nonlocal_part(c, j, list(split(current)), 0)
            half, inner = divmod(j, HALF)
            upstream_x = up_rows[pl.ds(half * local * HALF + inner, local, stride=HALF), :]
            upstream_y = jnp.where(vertical > 0, own_column(c, j - 1), own_column(c, j + 1))
            drift_x = -speed_ref[...] * (current - upstream_x)
            drift_y = -jnp.abs(vertical) * (current - upstream_y)
            column = pl.ds(c * WIDTH + j, 1)
            relaxation = rate[column, :] * (dens[column, :] * eq_ref[...] - current)
            total = current + STEP * (drift_x + drift_y + wigner + relaxation)
            out_rows[pl.ds(c * WIDTH + j, local, stride=cols), :] = total

        for h, half in enumerate(halves):
            for p in range(1, groups):
                spread_copy(p, c, half).wait_recv()
            count = WIDTH // len(halves)
            for j in range(h * count, (h + 1) * count):
                every = []
                for p in range(groups - 1):
                    start = (p * chunks + c) * (local * WIDTH) + j
                    every.append(spread_rows[pl.ds(start, local, stride=WIDTH), :])
                others = list(split(jnp.concatenate(every, axis=0)))
                wigner = nonlocal_part(c, j, others, local)
                place = pl.ds(c * WIDTH + j, local, stride=cols)
                out_rows[place, :] = out_rows[place, :] + STEP * wigner

    @pl.loop(0, last)
    def _(c):
        advance(c, (None,))

    advance(last, (0, 1))

    for p in range(1, groups):
        part_copy(p).wait_send()

        @pl.loop(0, last)
        def _(c):
            spread_copy(p, c).wait_send()

        for half in range(2):
            spread_copy(p, last, half).wait_send()

    @pl.loop(1, rows)
    def _(i):
        charge_copy(i).wait_send()

    @pl.loop(0, chunks)
    def _(c):
        @pl.when(row < rows - 1)
        def _():
            right_copy(c).wait_send()

        @pl.when(row > 0)
        def _():
            left_copy(c).wait_send()


def shards(rows, groups, distribution, region, doping, relax, equilibrium, speed, sign):
    _, local, cols, kx = distribution.shape
    modes = local * groups
    chunks = cols // WIDTH
    consts = tables(rows, groups, modes, cols)
    expand = consts[3].reshape(rows, rows, 8)
    order = (np.arange(rows)[:, None] - np.arange(rows)[None, :]) % rows
    consts[3] = np.stack([expand[:, order[r]].reshape(rows, rows * 8) for r in range(rows)])
    vmem = pl.BlockSpec(memory_space=pltpu.VMEM)
    smem = pl.BlockSpec(memory_space=pltpu.SMEM)
    hbm = pl.BlockSpec(memory_space=pl.ANY)
    piece = (local, WIDTH, kx)
    halo = (chunks, local, HALF, kx)
    dma = pltpu.SemaphoreType.DMA
    return pl.pallas_call(
        functools.partial(kernel, rows, groups),
        out_shape=pltpu.VMEM(distribution.shape, F32),
        in_specs=[hbm, vmem, smem, smem] + [vmem] * 3 + [hbm] * len(consts),
        out_specs=vmem,
        scratch_shapes=[pltpu.VMEM(t.shape, F32) for t in consts] + [
            pltpu.VMEM((chunks + 2,) + piece, F32),
            pltpu.VMEM((groups - 1, chunks) + piece, F32),
            pltpu.VMEM(halo, F32),
            pltpu.VMEM(halo, F32),
            pltpu.VMEM(halo, F32),
            pltpu.VMEM(halo, F32),
            pltpu.VMEM((chunks, local * WIDTH, modes), BF16),
            pltpu.VMEM((chunks, local * WIDTH, modes), BF16),
            pltpu.VMEM((cols, kx), F32),
            pltpu.VMEM((groups, 8, cols), F32),
            pltpu.VMEM((rows, 8, cols), F32),
            pltpu.VMEM((cols, modes), F32),
            pltpu.VMEM((cols, kx), F32),
            pltpu.VMEM((cols, kx), F32),
            pltpu.VMEM((2, local, HALF, kx), F32),
            dma((chunks,)),
            dma((groups - 1, chunks + 1)),
            dma((groups - 1, chunks + 1)),
            dma((groups - 1,)),
            dma((groups - 1,)),
            dma((rows - 1,)),
            dma((rows - 1,)),
            dma((chunks,)),
            dma((chunks,)),
            dma((chunks,)),
            dma((chunks,)),
            dma((len(consts),)),
        ],
        compiler_params=pltpu.CompilerParams(
            collective_id=0, has_side_effects=True, vmem_limit_bytes=52 * 1024 * 1024
        ),
        cost_estimate=pl.CostEstimate(
            flops=2 * modes * local * cols * kx * 6,
            bytes_accessed=8 * local * cols * kx,
            transcendentals=0,
        ),
    )(
        distribution, region, doping, relax, equilibrium,
        speed.reshape(1, kx), sign.reshape(1, kx), *consts,
    )


def solution(mesh):
    return jax.shard_map(
        functools.partial(shards, mesh.shape["space"], mesh.shape["ky"]),
        mesh=mesh,
        in_specs=(
            P("space", "ky", None, None),
            P("space", None),
            P(),
            P(),
            P("ky", None),
            P(),
            P(),
        ),
        out_specs=P("space", "ky", None, None),
        check_vma=False,
    )
```

```python
import functools

import jax
import jax.numpy as jnp
import numpy as np
from jax import lax
from jax.experimental import pallas as pl
from jax.experimental.pallas import tpu as pltpu
from jax.sharding import PartitionSpec as P

COUPLING = 0.04
POISSON = 0.1
STEP = 0.4
DRIFT_Y = 0.8
WIDTH = 16
HALF = WIDTH // 2
EARLY = 2
TABLES = 9
MESH = pl.DeviceIdType.MESH
BF16 = jnp.bfloat16
F32 = jnp.float32


def sine_table(length):
    positions = np.arange(1, length + 1)
    phase = positions[:, None] * positions[None, :] % (2 * length + 2)
    return np.sqrt(2.0 / (length + 1.0)) * np.sin(np.pi * phase / (length + 1.0))


def eigen_values(length):
    positions = np.arange(1, length + 1)
    return 4.0 * np.sin(0.5 * np.pi * positions / (length + 1.0)) ** 2


def tables(rows, groups, modes, cols):
    half = modes // 2
    local = modes // groups
    phase = np.arange(1, half + 1)[:, None] * np.arange(modes)[None, :] % modes
    angles = 2.0 * np.pi / modes * phase
    forward = np.concatenate([np.cos(angles), np.sin(angles)], axis=0)
    backward = np.concatenate([np.sin(angles).T, -np.cos(angles).T], axis=1)
    by_owner = forward.reshape(modes, groups, local)
    forward_of = np.stack(
        [
            np.concatenate([by_owner[:, (g - p) % groups] for p in range(groups)], axis=1)
            for g in range(groups)
        ]
    )
    backward_of = backward.reshape(groups, local, modes)
    speed = DRIFT_Y * (np.arange(modes) + 0.5 - 0.5 * modes) / (0.5 * modes)
    speed_of = np.broadcast_to(speed.reshape(groups, local, 1), (groups, local, 128))
    sine_rows = sine_table(rows)
    expand = np.zeros((rows, rows, 8))
    expand[:, :, 0] = sine_rows
    own_row = np.broadcast_to(sine_rows[:, None, :], (rows, 8, rows))
    sine_cols = sine_table(cols)
    padded = np.pad(sine_cols, ((0, 0), (half, half)))
    pick = np.zeros((cols + 2 * half, 2 * half))
    centre = cols - 1 + half
    for s in range(1, half + 1):
        for column in (s - 1, half + s - 1):
            pick[centre + s, column] = 1.0
            pick[centre - s, column] = -1.0
    eigen = eigen_values(rows)[:, None] + eigen_values(cols)[None, :]
    every = (
        forward_of, backward_of, speed_of, expand.reshape(rows, rows * 8), own_row,
        sine_cols, padded, pick, eigen,
    )
    return [np.asarray(t, np.float32) for t in every]


def exact(a, b, contract=((1,), (0,))):
    return lax.dot_general(
        a, b, (contract, ((), ())), precision=lax.Precision.HIGHEST, preferred_element_type=F32
    )


def split(x):
    high = x.astype(BF16)
    return high, (x - high.astype(F32)).astype(BF16)


def triple(a, b):
    (a_high, a_low), (b_high, b_low) = a, b
    mul = functools.partial(jnp.dot, preferred_element_type=F32)
    return mul(a_high, b_high) + (mul(a_high, b_low) + mul(a_low, b_high))


def kernel(
    rows, groups,
    f_hbm, region_ref, doping_ref, relax_ref, eq_ref, speed_ref, sign_ref,
    *refs,
):
    table_sources, out_ref, table_refs = refs[:TABLES], refs[TABLES], refs[TABLES + 1:2 * TABLES + 1]
    (
        forward_ref, backward_ref, vertical_ref, expand_ref, own_row_ref,
        sine_ref, padded_ref, pick_ref, eigen_ref,
    ) = table_refs
    (
        f_vm, spread, to_left, to_right, from_left, from_right, weight_high, weight_low,
        sums, parts, charges, diffs, dens, rate, up_x,
        load_sem, spread_send, spread_recv, part_send, part_recv, charge_send, charge_recv,
        left_send, left_recv, right_send, right_recv, table_sem,
    ) = refs[2 * TABLES + 1:]
    _, local, cols, kx = f_hbm.shape
    modes = local * groups
    chunks = cols // WIDTH
    last = chunks - 1
    row = lax.axis_index("space")
    group = lax.axis_index("ky")

    def other_group(p):
        return (row, lax.rem(group + p, groups))

    def other_row(i):
        return (lax.rem(row + i, rows), group)

    barrier = pltpu.get_barrier_semaphore()
    for p in range(1, groups):
        pl.semaphore_signal(barrier, inc=1, device_id=other_group(p), device_id_type=MESH)

    @pl.loop(1, rows)
    def _(i):
        pl.semaphore_signal(barrier, inc=1, device_id=other_row(i), device_id_type=MESH)

    def load(c):
        return pltpu.make_async_copy(
            f_hbm.at[0, :, pl.ds(pl.multiple_of(c * WIDTH, WIDTH), WIDTH), :],
            f_vm.at[c + 1], load_sem.at[c],
        )

    @pl.loop(0, chunks)
    def _(c):
        load(c).start()

    pl.semaphore_wait(barrier, rows + groups - 2)

    def spread_copy(p, c, half=None):
        first_col = pl.multiple_of(c * WIDTH, WIDTH)
        place, target, sem = pl.ds(first_col, WIDTH), spread.at[p - 1, c], c
        if half is not None:
            place = pl.ds(last * WIDTH + half * HALF, HALF)
            target, sem = spread.at[p - 1, last, :, pl.ds(half * HALF, HALF), :], last + half
        return pltpu.make_async_remote_copy(
            src_ref=f_hbm.at[0, :, place, :],
            dst_ref=target,
            send_sem=spread_send.at[p - 1, sem], recv_sem=spread_recv.at[p - 1, sem],
            device_id=other_group(p), device_id_type=MESH,
        )

    def part_copy(p):
        return pltpu.make_async_remote_copy(
            src_ref=parts.at[0], dst_ref=parts.at[p],
            send_sem=part_send.at[p - 1], recv_sem=part_recv.at[p - 1],
            device_id=other_group(p), device_id_type=MESH,
        )

    def charge_copy(i):
        return pltpu.make_async_remote_copy(
            src_ref=charges.at[0], dst_ref=charges.at[i],
            send_sem=charge_send.at[i - 1], recv_sem=charge_recv.at[i - 1],
            device_id=other_row(i), device_id_type=MESH,
        )

    def right_copy(c):
        return pltpu.make_async_remote_copy(
            src_ref=to_right.at[c], dst_ref=from_left.at[c],
            send_sem=right_send.at[c], recv_sem=right_recv.at[c],
            device_id=other_row(1), device_id_type=MESH,
        )

    def left_copy(c):
        return pltpu.make_async_remote_copy(
            src_ref=to_left.at[c], dst_ref=from_right.at[c],
            send_sem=left_send.at[c], recv_sem=left_recv.at[c],
            device_id=other_row(rows - 1), device_id_type=MESH,
        )

    for c in range(min(EARLY, last)):
        for p in range(1, groups):
            spread_copy(p, c).start()

    table_copies = [
        pltpu.make_async_copy(source, table, table_sem.at[i])
        for i, (source, table) in enumerate(zip(table_sources, table_refs))
    ]
    for copy in table_copies:
        copy.start()

    blank = jnp.zeros(f_vm.shape[1:], F32)
    f_vm[0] = blank
    f_vm[chunks + 1] = blank

    @pl.loop(0, chunks)
    def _(c):
        load(c).wait()
        sums[pl.ds(pl.multiple_of(c * WIDTH, WIDTH), WIDTH), :] = jnp.sum(f_vm[c + 1], axis=0)

    parts[0] = exact(jnp.ones((8, kx), F32), sums[...], ((1,), (1,))) / (modes * kx)
    for p in range(1, groups):
        part_copy(p).start()

    @pl.loop(min(EARLY, last), last)
    def _(c):
        for p in range(1, groups):
            spread_copy(p, c).start()

    for half in range(2):
        for p in range(1, groups):
            spread_copy(p, last, half).start()

    lane = lax.broadcasted_iota(jnp.int32, (kx, kx), 1)
    place = lax.broadcasted_iota(jnp.int32, (kx, kx), 0)
    positive = jnp.broadcast_to(sign_ref[...] > 0, (kx, kx))
    ahead = exact(positive.astype(F32), (place < lane).astype(F32)).astype(jnp.int32)
    target = jnp.where(positive, ahead, kx // 2 + lane - ahead)
    first = (target == place).astype(F32)
    second = (lax.rem(target + kx // 2, kx) == place).astype(F32)
    low_lane = lax.broadcasted_iota(jnp.int32, (local * HALF, kx), 1) < kx // 2

    @pl.loop(0, chunks)
    def _(c):
        one = exact(f_vm[c + 1, :, :HALF, :].reshape(local * HALF, kx), first, ((1,), (1,)))
        two = exact(f_vm[c + 1, :, HALF:, :].reshape(local * HALF, kx), second, ((1,), (1,)))
        to_right[c] = jnp.where(low_lane, one, two).reshape(local, HALF, kx)
        to_left[c] = jnp.where(low_lane, two, one).reshape(local, HALF, kx)

    def lookup(table):
        region = jnp.broadcast_to(region_ref[...], (8, cols))
        value = jnp.zeros((8, cols), F32)
        for k in range(table.shape[0]):
            value = value + jnp.where(region == k, table[k], 0.0)
        return value

    def down(values):
        shape = (cols, cols)
        same = lax.broadcasted_iota(jnp.int32, shape, 0) == lax.broadcasted_iota(jnp.int32, shape, 1)
        spread_out = jnp.where(same, jnp.broadcast_to(values[:1], shape), 0.0)
        return exact(spread_out, jnp.ones((cols, kx), F32))

    rate[...] = down(lookup(relax_ref))
    for p in range(1, groups):
        part_copy(p).wait_recv()
    density = parts[0]
    for p in range(1, groups):
        density = density + parts[p]
    charges[0] = density - lookup(doping_ref)

    @pl.loop(1, rows)
    def _(i):
        charge_copy(i).start()

    @pl.loop(0, chunks)
    def _(c):
        @pl.when(row < rows - 1)
        def _():
            right_copy(c).start()

        @pl.when(row > 0)
        def _():
            left_copy(c).start()

    @pl.when(row == 0)
    def _():
        @pl.loop(0, chunks)
        def _(c):
            from_left[c] = jnp.zeros(from_left.shape[1:], F32)

    @pl.when(row == rows - 1)
    def _():
        @pl.loop(0, chunks)
        def _(c):
            from_right[c] = jnp.zeros(from_right.shape[1:], F32)

    dens[...] = down(density)
    for copy in table_copies:
        copy.wait()

    @pl.loop(1, rows)
    def _(i):
        charge_copy(i).wait_recv()

    along_x = exact(expand_ref[row], charges[...].reshape(rows * 8, cols))
    spectral = exact(along_x, sine_ref[...]) / eigen_ref[...]
    own = exact(own_row_ref[row], spectral)
    potential = POISSON * exact(own, padded_ref[...])
    wide = jnp.broadcast_to(potential[:1], (cols, potential.shape[1]))
    shifted = pltpu.roll(wide, 0, 1, stride=1, stride_axis=0)
    diffs[...] = COUPLING * exact(shifted, pick_ref[...])

    forward = split(forward_ref[group])

    @pl.loop(0, chunks)
    def _(c):
        scaled = []
        for j in range(WIDTH):
            weights = diffs[pl.ds(cols - 1 - (c * WIDTH + j), 1), :]
            scaled.append(backward_ref[group] * weights)
        table = triple(split(jnp.concatenate(scaled, axis=0)), forward)
        high, low = split(table)
        weight_high[c] = high
        weight_low[c] = low

    f_rows = f_vm.reshape((chunks + 2) * local * WIDTH, kx)
    spread_rows = spread.reshape((groups - 1) * chunks * local * WIDTH, kx)
    up_rows = up_x.reshape(2 * local * HALF, kx)
    out_rows = out_ref.reshape(local * cols, kx)

    def nonlocal_part(c, j, values, start):
        count = values[0].shape[0]
        blank_before = [jnp.zeros((start, kx), BF16)] if start else []
        rest = modes - start - count
        blank_after = [jnp.zeros((rest, kx), BF16)] if rest else []
        padded = [jnp.concatenate(blank_before + [v] + blank_after, axis=0) for v in values]
        picked = pl.ds(j * local, local)
        return triple((weight_high[c, picked, :], weight_low[c, picked, :]), padded)

    def own_column(c, j):
        c, j = (c - 1, WIDTH - 1) if j < 0 else (c + 1, 0) if j == WIDTH else (c, j)
        return f_rows[pl.ds((c + 1) * (local * WIDTH) + j, local, stride=WIDTH), :]

    def advance(c, halves):
        @pl.when(row > 0)
        def _():
            right_copy(c).wait_recv()

        @pl.when(row < rows - 1)
        def _():
            left_copy(c).wait_recv()

        left = from_left[c].reshape(local * HALF, kx)
        right = from_right[c].reshape(local * HALF, kx)
        up_x[0] = exact(jnp.where(low_lane, left, right), first).reshape(local, HALF, kx)
        up_x[1] = exact(jnp.where(low_lane, right, left), second).reshape(local, HALF, kx)

        vertical = vertical_ref[group]
        for j in range(WIDTH):
            current = own_column(c, j)
            wigner = nonlocal_part(c, j, list(split(current)), 0)
            half, inner = divmod(j, HALF)
            upstream_x = up_rows[pl.ds(half * local * HALF + inner, local, stride=HALF), :]
            upstream_y = jnp.where(vertical > 0, own_column(c, j - 1), own_column(c, j + 1))
            drift_x = -speed_ref[...] * (current - upstream_x)
            drift_y = -jnp.abs(vertical) * (current - upstream_y)
            column = pl.ds(c * WIDTH + j, 1)
            relaxation = rate[column, :] * (dens[column, :] * eq_ref[...] - current)
            total = current + STEP * (drift_x + drift_y + wigner + relaxation)
            out_rows[pl.ds(c * WIDTH + j, local, stride=cols), :] = total

        for h, half in enumerate(halves):
            for p in range(1, groups):
                spread_copy(p, c, half).wait_recv()
            count = WIDTH // len(halves)
            for j in range(h * count, (h + 1) * count):
                every = []
                for p in range(groups - 1):
                    start = (p * chunks + c) * (local * WIDTH) + j
                    every.append(spread_rows[pl.ds(start, local, stride=WIDTH), :])
                others = list(split(jnp.concatenate(every, axis=0)))
                wigner = nonlocal_part(c, j, others, local)
                place = pl.ds(c * WIDTH + j, local, stride=cols)
                out_rows[place, :] = out_rows[place, :] + STEP * wigner

    @pl.loop(0, last)
    def _(c):
        advance(c, (None,))

    for p in range(1, groups):
        part_copy(p).wait_send()

        @pl.loop(0, last)
        def _(c):
            spread_copy(p, c).wait_send()

    @pl.loop(1, rows)
    def _(i):
        charge_copy(i).wait_send()

    @pl.loop(0, chunks)
    def _(c):
        @pl.when(row < rows - 1)
        def _():
            right_copy(c).wait_send()

        @pl.when(row > 0)
        def _():
            left_copy(c).wait_send()

    advance(last, (0, 1))

    for p in range(1, groups):
        for half in range(2):
            spread_copy(p, last, half).wait_send()


def shards(rows, groups, distribution, region, doping, relax, equilibrium, speed, sign):
    _, local, cols, kx = distribution.shape
    modes = local * groups
    chunks = cols // WIDTH
    consts = tables(rows, groups, modes, cols)
    expand = consts[3].reshape(rows, rows, 8)
    order = (np.arange(rows)[:, None] - np.arange(rows)[None, :]) % rows
    consts[3] = np.stack([expand[:, order[r]].reshape(rows, rows * 8) for r in range(rows)])
    vmem = pl.BlockSpec(memory_space=pltpu.VMEM)
    smem = pl.BlockSpec(memory_space=pltpu.SMEM)
    hbm = pl.BlockSpec(memory_space=pl.ANY)
    piece = (local, WIDTH, kx)
    halo = (chunks, local, HALF, kx)
    dma = pltpu.SemaphoreType.DMA
    return pl.pallas_call(
        functools.partial(kernel, rows, groups),
        out_shape=pltpu.VMEM(distribution.shape, F32),
        in_specs=[hbm, vmem, smem, smem] + [vmem] * 3 + [hbm] * len(consts),
        out_specs=vmem,
        scratch_shapes=[pltpu.VMEM(t.shape, F32) for t in consts] + [
            pltpu.VMEM((chunks + 2,) + piece, F32),
            pltpu.VMEM((groups - 1, chunks) + piece, F32),
            pltpu.VMEM(halo, F32),
            pltpu.VMEM(halo, F32),
            pltpu.VMEM(halo, F32),
            pltpu.VMEM(halo, F32),
            pltpu.VMEM((chunks, local * WIDTH, modes), BF16),
            pltpu.VMEM((chunks, local * WIDTH, modes), BF16),
            pltpu.VMEM((cols, kx), F32),
            pltpu.VMEM((groups, 8, cols), F32),
            pltpu.VMEM((rows, 8, cols), F32),
            pltpu.VMEM((cols, modes), F32),
            pltpu.VMEM((cols, kx), F32),
            pltpu.VMEM((cols, kx), F32),
            pltpu.VMEM((2, local, HALF, kx), F32),
            dma((chunks,)),
            dma((groups - 1, chunks + 1)),
            dma((groups - 1, chunks + 1)),
            dma((groups - 1,)),
            dma((groups - 1,)),
            dma((rows - 1,)),
            dma((rows - 1,)),
            dma((chunks,)),
            dma((chunks,)),
            dma((chunks,)),
            dma((chunks,)),
            dma((len(consts),)),
        ],
        compiler_params=pltpu.CompilerParams(
            collective_id=0, has_side_effects=True, vmem_limit_bytes=52 * 1024 * 1024
        ),
        cost_estimate=pl.CostEstimate(
            flops=2 * modes * local * cols * kx * 6,
            bytes_accessed=8 * local * cols * kx,
            transcendentals=0,
        ),
    )(
        distribution, region, doping, relax, equilibrium,
        speed.reshape(1, kx), sign.reshape(1, kx), *consts,
    )


def solution(mesh):
    return jax.shard_map(
        functools.partial(shards, mesh.shape["space"], mesh.shape["ky"]),
        mesh=mesh,
        in_specs=(
            P("space", "ky", None, None),
            P("space", None),
            P(),
            P(),
            P("ky", None),
            P(),
            P(),
        ),
        out_specs=P("space", "ky", None, None),
        check_vma=False,
    )
```
